32 devices in a mesh: grp: 2 (over y), wloop: 4 (over z), head: 4 (over x, core).
Axes of the slice: x: 2, y: 2, z: 4, core: 2. Of those that a mesh axis runs over, the one named last changes fastest.
Arguments:
- tokens: bfloat16 [4096, 8192], P(('grp', 'wloop'), 'head'), parts along dimension 0, may hold values from -200 to 200
- norm_gain: float32 [8192], replicated, may hold values from 0.1 to 1.9
- w_query: bfloat16 [8192, 8192], P('wloop', 'head'), may hold values from -0.0625 to 0.0625
- w_key: bfloat16 [8192, 1024], P('wloop', 'head'), may hold values from -0.0625 to 0.0625
- w_value: bfloat16 [8192, 1024], P('wloop', 'head'), may hold values from -0.0625 to 0.0625
- cache_key: bfloat16 [32, 1024, 1024], P(('grp', 'wloop'), None, 'head'), parts along dimension 0, may hold values from -600 to 600
- cache_value: bfloat16 [32, 1024, 1024], P(('grp', 'wloop'), None, 'head'), parts along dimension 0, may hold values from -6 to 6
- turn_len: int32 [32], P(('grp', 'wloop')), parts along dimension 0, may hold values from 1 to 128, as said below
- cache_len: int32 [32], P(('grp', 'wloop')), parts along dimension 0, may hold values from 1 to 1024, as said below
Outputs:
- attended: bfloat16 [4096, 8192], P(('grp', 'wloop'), 'head'), parts along dimension 0
- fresh_keys: bfloat16 [4096, 1024], P(('grp', 'wloop'), 'head'), parts along dimension 0
- fresh_values: bfloat16 [4096, 1024], P(('grp', 'wloop'), 'head'), parts along dimension 0
The draws below stay inside these ranges and needn't reach their ends.
There are 2 independent parts, one for each index of `grp`. The reference program is written for one: setup_inputs(seed, part) draws one part's arguments, and reference() takes and returns one part's arrays. A program takes and returns all parts, laid end to end along the dimension named above; an argument that names none is the same for every part. Nothing has to cross between parts.
Inputs may be any that keep to these rules, and one draw needn't show every extreme that they name: Session s owns rows s * 128 to s * 128 + 127 of tokens; the first turn_len[s] of them are live, the rest padding. Slots 0 to cache_len[s] - 1 of session s's cache are filled, the others are padding; the new turn's positions follow the cached prefix.
All inputs are finite; a program needn't handle non-finite values.
Results may differ from the reference program's by a relative error of at most 0.012.
The reference program's roundings to bfloat16 on the way count: a program that leaves them out, or rounds other values in their place, can miss the bound.
Values may be sent and summed in bfloat16 or wider, within the bound.
A program may use at most 192 MiB of HBM per device.

```python
import math
import jax
import jax.numpy as jnp
from jax import lax

D = 8192
HEADS = 64
KV_HEADS = 8
HEAD_DIM = 128
S_DEV = 4
CACHE = 1024
TURN = 128
SESSIONS = 16
TOKENS = 2048


def spread_lengths(key, largest):
    groups = SESSIONS // S_DEV
    key_cap, key_chosen, key_counts, key_picked = jax.random.split(key, 4)
    ceiling = jax.random.randint(key_cap, (groups, 1), largest // 4, largest + 1)
    chosen = jax.random.randint(key_chosen, (), 0, groups)
    ceiling = jnp.where(jnp.arange(groups)[:, None] == chosen, largest, ceiling)
    counts = jax.random.randint(key_counts, (groups, S_DEV), ceiling // 2, ceiling + 1)
    picked = jax.random.randint(key_picked, (groups, 1), 0, S_DEV)
    counts = jnp.where(jnp.arange(S_DEV)[None, :] == picked, ceiling, counts)
    return counts.reshape(SESSIONS).astype(jnp.int32)


def draw_turn_len(key, part):
    key = jax.random.fold_in(key, 5)
    return spread_lengths(key, TURN)


def draw_cache_len(key, part):
    key = jax.random.fold_in(key, 7)
    return spread_lengths(key, CACHE)


def draw_tokens(key, part):
    key = jax.random.fold_in(key, 11)
    key_rows, key_cols, key_base = jax.random.split(key, 3)
    row_scale = jnp.exp(jax.random.uniform(key_rows, (TOKENS, 1), jnp.float32) * math.log(10.0))
    col_scale = jnp.exp(jax.random.uniform(key_cols, (1, D), jnp.float32) * math.log(10.0))
    base = jnp.clip(jax.random.normal(key_base, (TOKENS, D), jnp.float32), -6.0, 6.0)
    return (0.3 * base * row_scale * col_scale).astype(jnp.bfloat16)


def draw_cache_key(key, part):
    key = jax.random.fold_in(key, 13)
    key_base = jax.random.fold_in(key, 0)
    width = KV_HEADS * HEAD_DIM
    base = jnp.clip(jax.random.normal(key_base, (SESSIONS, CACHE, width), jnp.float32), -6.0, 6.0)
    return base.astype(jnp.bfloat16)


def shard_levels(own_key, shape, shards, smallest, high):
    def one(axis_at, parts):
        heights = jax.random.uniform(jax.random.fold_in(jax.random.fold_in(own_key, 6), axis_at), (parts,), jnp.float32, smallest / len(shards), high / len(shards))
        return jnp.repeat(jnp.exp(heights), shape[axis_at] // parts).reshape((-1,) + (1,) * (len(shape) - axis_at - 1))

    loudness = one(*shards[0])
    for cut in shards[1:]:
        loudness = loudness * one(*cut)
    return loudness


def centred(own_key, extent, scale, limit, cuts=(), held_as=jnp.bfloat16):
    gain = shard_levels(own_key, extent, cuts, -0.22, 0.18) if cuts else 1.0
    values = jax.random.normal(own_key, extent, jnp.float32) * scale * gain
    return jnp.minimum(jnp.maximum(values, -limit), limit).astype(held_as)


def setup_inputs(seed: int = 0, part: int = 0) -> dict:
    arg_keys = jax.random.split(jax.random.key(seed), 10)
    part_splits = jax.random.split(jax.random.fold_in(arg_keys[9], part), 10)
    tokens = draw_tokens(jax.random.fold_in(jax.random.fold_in(arg_keys[9], part), 71), part)
    norm_gain = jnp.clip(1.0 + 0.18 * jax.random.normal(arg_keys[1], (D,), jnp.float32), 0.1, 1.9)
    w_query = centred(arg_keys[2], (D, HEADS * HEAD_DIM), D ** -0.5, 0.0625, ((0, 4), (1, 4)))
    w_key = centred(arg_keys[3], (D, KV_HEADS * HEAD_DIM), D ** -0.5, 0.0625, ((0, 4), (1, 4)))
    w_value = centred(arg_keys[4], (D, KV_HEADS * HEAD_DIM), D ** -0.5, 0.0625, ((0, 4), (1, 4)))
    cache_key = draw_cache_key(jax.random.fold_in(jax.random.fold_in(arg_keys[9], part), 71), part)
    cache_value = centred(part_splits[6], (SESSIONS, CACHE, KV_HEADS * HEAD_DIM), 1.0, 6.0, ((0, 4), (2, 4)))
    turn_len = draw_turn_len(jax.random.fold_in(jax.random.fold_in(arg_keys[9], part), 71), part)
    cache_len = draw_cache_len(jax.random.fold_in(jax.random.fold_in(arg_keys[9], part), 71), part)
    return dict(tokens=tokens, norm_gain=norm_gain, w_query=w_query, w_key=w_key, w_value=w_value, cache_key=cache_key, cache_value=cache_value, turn_len=turn_len, cache_len=cache_len)


EPSILON = 1e-06
THETA = 1000000.0

def rotate(vectors, positions):
    half_dim = vectors.shape[-1] // 2
    freq_index = jnp.arange(half_dim, dtype=jnp.float32)
    frequency = jnp.power(jnp.float32(THETA), freq_index * (-2.0 / vectors.shape[-1]))
    angles = positions[..., None] * frequency
    cosine = jnp.cos(angles)
    sine_part = jnp.sin(angles)
    lower_half = vectors[..., :half_dim]
    upper_half = vectors[..., half_dim:]
    return jnp.concatenate([lower_half * cosine - upper_half * sine_part, upper_half * cosine + lower_half * sine_part], axis=-1)

def attend(operands):
    rotated, new_keys, new_values, old_keys, old_values, turn_count, cache_count = operands
    turn_size, head_count, head_dim = rotated.shape
    kv_count = old_keys.shape[1]
    group_size = head_count // kv_count
    cache_size = old_keys.shape[0]
    factor = head_dim ** (-0.5)
    grouped = rotated.reshape(turn_size, kv_count, group_size, head_dim).astype(jnp.float32)
    far_scores = jnp.einsum('tkgd,lkd->kgtl', grouped, old_keys.astype(jnp.float32)) * factor
    near_scores = jnp.einsum('tkgd,ukd->kgtu', grouped, new_keys.astype(jnp.float32)) * factor
    slot_index = jnp.arange(cache_size, dtype=jnp.int32)
    turn_index = jnp.arange(turn_size, dtype=jnp.int32)
    far_scores = jnp.where(slot_index < cache_count, far_scores, -jnp.inf)
    near_scores = jnp.where(turn_index[None, :] <= turn_index[:, None], near_scores, -jnp.inf)
    row_max = jnp.maximum(lax.optimization_barrier(jnp.max(far_scores, axis=-1)), lax.optimization_barrier(jnp.max(near_scores, axis=-1)))[..., None]
    far_exp = jnp.exp(far_scores - row_max)
    near_exp = jnp.exp(near_scores - row_max)
    totals = lax.optimization_barrier(jnp.sum(far_exp, axis=-1, keepdims=True)) + lax.optimization_barrier(jnp.sum(near_exp, axis=-1, keepdims=True))
    far_weights = (far_exp / totals).astype(jnp.bfloat16)
    near_weights = (near_exp / totals).astype(jnp.bfloat16)
    mixed = jnp.einsum('kgtl,lkd->tkgd', far_weights.astype(jnp.float32), old_values.astype(jnp.float32))
    mixed = mixed + jnp.einsum('kgtu,ukd->tkgd', near_weights.astype(jnp.float32), new_values.astype(jnp.float32))
    mixed = jnp.where((turn_index < turn_count)[:, None, None, None], mixed, 0.0)
    return mixed.reshape(turn_size, head_count * head_dim).astype(jnp.bfloat16)

def reference(tokens, norm_gain, w_query, w_key, w_value, cache_key, cache_value, turn_len, cache_len):
    widened = tokens.astype(jnp.float32)
    inverse_rms = lax.rsqrt(lax.optimization_barrier(jnp.mean(widened * widened, axis=1, keepdims=True)) + EPSILON)
    normed = (widened * inverse_rms * norm_gain).astype(jnp.bfloat16)
    queries = jnp.dot(normed, w_query, preferred_element_type=jnp.float32)
    keys_raw = jnp.dot(normed, w_key, preferred_element_type=jnp.float32)
    values_raw = jnp.dot(normed, w_value, preferred_element_type=jnp.float32)
    session_count = turn_len.shape[0]
    turn_index = jnp.arange(TURN, dtype=jnp.int32)
    positions = (cache_len[:, None] + turn_index[None, :]).astype(jnp.float32)[:, :, None]
    live_rows = turn_index[None, :] < turn_len[:, None]
    rotated = rotate(queries.reshape(session_count, TURN, HEADS, HEAD_DIM), positions).astype(jnp.bfloat16)
    new_keys = jnp.where(live_rows[:, :, None, None], rotate(keys_raw.reshape(session_count, TURN, KV_HEADS, HEAD_DIM), positions), 0.0).astype(jnp.bfloat16)
    new_values = jnp.where(live_rows[:, :, None, None], values_raw.reshape(session_count, TURN, KV_HEADS, HEAD_DIM), 0.0).astype(jnp.bfloat16)
    old_keys = cache_key.reshape(session_count, CACHE, KV_HEADS, HEAD_DIM)
    old_values = cache_value.reshape(session_count, CACHE, KV_HEADS, HEAD_DIM)
    attended = lax.map(attend, (rotated, new_keys, new_values, old_keys, old_values, turn_len, cache_len))
    return (attended.reshape(TOKENS, HEADS * HEAD_DIM), new_keys.reshape(TOKENS, KV_HEADS * HEAD_DIM), new_values.reshape(TOKENS, KV_HEADS * HEAD_DIM))
```

```python
import jax
import jax.numpy as jnp
from jax import lax
from jax.sharding import PartitionSpec as P

HEAD_DIM = 128


EPSILON = 1e-06
THETA = 1000000.0


def rotate(vectors, positions):
    half_dim = vectors.shape[-1] // 2
    freq_index = jnp.arange(half_dim, dtype=jnp.float32)
    frequency = jnp.power(jnp.float32(THETA), freq_index * (-2.0 / vectors.shape[-1]))
    angles = positions[..., None] * frequency
    cosine = jnp.cos(angles)
    sine_part = jnp.sin(angles)
    lower_half = vectors[..., :half_dim]
    upper_half = vectors[..., half_dim:]
    return jnp.concatenate(
        [
            lower_half * cosine - upper_half * sine_part,
            upper_half * cosine + lower_half * sine_part,
        ],
        axis=-1,
    )


def project_rows(normed, weight_rows):
    return jnp.dot(normed, weight_rows, preferred_element_type=jnp.float32)


def attend_all(rotated, new_keys, new_values, old_keys, old_values, turn_len, cache_len):
    session_count, turn_size, kv_local, head_dim = new_keys.shape
    head_local = rotated.shape[2]
    group_size = head_local // kv_local
    cache_size = old_keys.shape[1]
    factor = head_dim ** (-0.5)
    grouped = rotated.reshape(session_count, turn_size, kv_local, group_size, head_dim)
    far_scores = (
        jnp.einsum("stkgd,slkd->skgtl", grouped, old_keys, preferred_element_type=jnp.float32)
        * factor
    )
    near_scores = (
        jnp.einsum("stkgd,sukd->skgtu", grouped, new_keys, preferred_element_type=jnp.float32)
        * factor
    )
    slot_index = jnp.arange(cache_size, dtype=jnp.int32)
    turn_index = jnp.arange(turn_size, dtype=jnp.int32)
    slot_live = slot_index[None, :] < cache_len[:, None]
    far_scores = jnp.where(slot_live[:, None, None, None, :], far_scores, -jnp.inf)
    near_scores = jnp.where(turn_index[None, :] <= turn_index[:, None], near_scores, -jnp.inf)
    row_max = jnp.maximum(jnp.max(far_scores, axis=-1), jnp.max(near_scores, axis=-1))[..., None]
    far_exp = jnp.exp(far_scores - row_max)
    near_exp = jnp.exp(near_scores - row_max)
    totals = jnp.sum(far_exp, axis=-1, keepdims=True) + jnp.sum(near_exp, axis=-1, keepdims=True)
    far_weights = (far_exp / totals).astype(jnp.bfloat16)
    near_weights = (near_exp / totals).astype(jnp.bfloat16)
    mixed = jnp.einsum(
        "skgtl,slkd->stkgd", far_weights, old_values, preferred_element_type=jnp.float32
    )
    mixed = mixed + jnp.einsum(
        "skgtu,sukd->stkgd", near_weights, new_values, preferred_element_type=jnp.float32
    )
    live_rows = turn_index[None, :] < turn_len[:, None]
    mixed = jnp.where(live_rows[:, :, None, None, None], mixed, 0.0)
    return mixed.reshape(session_count * turn_size, head_local * head_dim).astype(jnp.bfloat16)


def local_gather(tokens, norm_gain, w_query, w_key, w_value, cache_key, cache_value, turn_len, cache_len):
    gathered = lax.all_gather(tokens, "head", axis=1, tiled=True)
    widened = gathered.astype(jnp.float32)
    inverse_rms = lax.rsqrt(jnp.mean(widened * widened, axis=1, keepdims=True) + EPSILON)
    normed = (widened * inverse_rms * norm_gain).astype(jnp.bfloat16)
    row_count = normed.shape[0]
    query_width = w_query.shape[1]
    pair_width = w_key.shape[1]
    queries = project_rows(normed, lax.all_gather(w_query, "wloop", axis=0, tiled=True))
    keys_raw = project_rows(normed, lax.all_gather(w_key, "wloop", axis=0, tiled=True))
    values_raw = project_rows(normed, lax.all_gather(w_value, "wloop", axis=0, tiled=True))
    session_count = turn_len.shape[0]
    turn_size = row_count // session_count
    head_local = query_width // HEAD_DIM
    kv_local = pair_width // HEAD_DIM
    turn_index = jnp.arange(turn_size, dtype=jnp.int32)
    positions = (cache_len[:, None] + turn_index[None, :]).astype(jnp.float32)[:, :, None]
    live_rows = turn_index[None, :] < turn_len[:, None]
    rotated = rotate(
        queries.reshape(session_count, turn_size, head_local, HEAD_DIM), positions
    ).astype(jnp.bfloat16)
    new_keys = jnp.where(
        live_rows[:, :, None, None],
        rotate(keys_raw.reshape(session_count, turn_size, kv_local, HEAD_DIM), positions),
        0.0,
    ).astype(jnp.bfloat16)
    new_values = jnp.where(
        live_rows[:, :, None, None],
        values_raw.reshape(session_count, turn_size, kv_local, HEAD_DIM),
        0.0,
    ).astype(jnp.bfloat16)
    old_keys = cache_key.reshape(session_count, cache_key.shape[1], kv_local, HEAD_DIM)
    old_values = cache_value.reshape(session_count, cache_value.shape[1], kv_local, HEAD_DIM)
    attended = attend_all(rotated, new_keys, new_values, old_keys, old_values, turn_len, cache_len)
    return (
        attended,
        new_keys.reshape(row_count, pair_width),
        new_values.reshape(row_count, pair_width),
    )


def transposed_tokens(tokens, ways):
    row_count = tokens.shape[0]
    session_rows = row_count // ways
    w_at = lax.axis_index("wloop")
    h_at = lax.axis_index("head")
    received = []
    for shift in range(ways):
        target = lax.rem(w_at + shift, ways)
        piece = lax.dynamic_slice_in_dim(tokens, target * session_rows, session_rows, 0)
        pairs = [
            (w * ways + h, h * ways + (w + shift) % ways) for w in range(ways) for h in range(ways)
        ]
        received.append(lax.ppermute(piece, ("wloop", "head"), pairs))
    stacked = jnp.stack(received)
    order = lax.rem(h_at + ways - jnp.arange(ways), ways)
    own_rows = jnp.take(stacked, order, axis=0)
    return lax.all_gather(own_rows, "head", axis=0)


def reduce_over_line(partials, ways):
    w_at = lax.axis_index("wloop")

    def pick(index):
        return lax.dynamic_index_in_dim(
            partials, jnp.clip(index, 0, ways - 1), 0, keepdims=False
        )

    rising = None
    falling = None
    for step in range(1, ways):
        up = pick(w_at + ways - step)
        down = pick(w_at - ways + step)
        if rising is not None:
            up = up + rising.astype(jnp.float32)
            down = down + falling.astype(jnp.float32)
        rising = lax.ppermute(
            up.astype(jnp.bfloat16), "wloop", [(w, w + 1) for w in range(step)]
        )
        falling = lax.ppermute(
            down.astype(jnp.bfloat16), "wloop", [(ways - 1 - w, ways - 2 - w) for w in range(step)]
        )
    return pick(w_at) + rising.astype(jnp.float32) + falling.astype(jnp.float32)


def local_reduce(
    tokens, norm_gain, w_query, w_key, w_value, cache_key, cache_value, turn_len, cache_len
):
    ways = lax.axis_size("wloop")
    row_count = tokens.shape[0]
    depth = w_query.shape[0]
    width = norm_gain.shape[0]
    kv_local = w_key.shape[1] // HEAD_DIM
    head_local = w_query.shape[1] // HEAD_DIM
    group_size = head_local // kv_local
    session_count = turn_len.shape[0]
    turn_size = row_count // session_count
    cache_size = cache_key.shape[1]
    w_at = lax.axis_index("wloop")

    widened = tokens.astype(jnp.float32)
    squares = jnp.sum(widened * widened, axis=1)
    all_squares = lax.all_gather(squares, ("wloop", "head"), axis=0)
    mean = jnp.sum(all_squares.reshape(ways, ways, row_count), axis=1) / width
    inverse_rms = lax.rsqrt(mean + EPSILON).reshape(ways, ways, row_count // ways)
    inverse_rms = jnp.transpose(inverse_rms, (1, 0, 2))

    gathered = transposed_tokens(tokens, ways)
    gain = lax.dynamic_slice_in_dim(norm_gain, w_at * depth, depth, 0)
    normed = (gathered.astype(jnp.float32) * inverse_rms[..., None] * gain).astype(jnp.bfloat16)
    normed = jnp.transpose(normed, (1, 0, 2, 3)).reshape(ways, row_count, depth)

    turn_index = jnp.arange(turn_size, dtype=jnp.int32)
    positions = (cache_len[:, None] + turn_index[None, :]).astype(jnp.float32)[:, :, None]
    live_rows = turn_index[None, :] < turn_len[:, None]
    outs = []
    for kv in range(kv_local):
        q_cols = group_size * HEAD_DIM
        weights = jnp.concatenate(
            [
                w_query[:, kv * q_cols : (kv + 1) * q_cols],
                w_key[:, kv * HEAD_DIM : (kv + 1) * HEAD_DIM],
                w_value[:, kv * HEAD_DIM : (kv + 1) * HEAD_DIM],
            ],
            axis=1,
        )
        partials = jnp.einsum("brd,dn->brn", normed, weights, preferred_element_type=jnp.float32)
        summed = reduce_over_line(partials, ways)
        queries = summed[:, :q_cols]
        keys_raw = summed[:, q_cols : q_cols + HEAD_DIM]
        values_raw = summed[:, q_cols + HEAD_DIM :]
        rotated = rotate(
            queries.reshape(session_count, turn_size, group_size, HEAD_DIM), positions
        ).astype(jnp.bfloat16)
        new_keys = jnp.where(
            live_rows[:, :, None, None],
            rotate(keys_raw.reshape(session_count, turn_size, 1, HEAD_DIM), positions),
            0.0,
        ).astype(jnp.bfloat16)
        new_values = jnp.where(
            live_rows[:, :, None, None],
            values_raw.reshape(session_count, turn_size, 1, HEAD_DIM),
            0.0,
        ).astype(jnp.bfloat16)
        old_keys = cache_key[:, :, kv * HEAD_DIM : (kv + 1) * HEAD_DIM][:, :, None, :]
        old_values = cache_value[:, :, kv * HEAD_DIM : (kv + 1) * HEAD_DIM][:, :, None, :]
        attended = attend_all(
            rotated, new_keys, new_values, old_keys, old_values, turn_len, cache_len
        )
        outs.append(
            (attended, new_keys.reshape(row_count, -1), new_values.reshape(row_count, -1))
        )
    return tuple(jnp.concatenate(arrays, axis=1) for arrays in zip(*outs))


def local(*args):
    tokens, norm_gain = args[0], args[1]
    w_ways, h_ways = lax.axis_size("wloop"), lax.axis_size("head")
    if w_ways == h_ways and w_ways > 1 and tokens.shape[0] % w_ways == 0:
        if w_ways * tokens.shape[0] < norm_gain.shape[0]:
            return local_reduce(*args)
    return local_gather(*args)


def solution(mesh):
    placed = (
        P(("grp", "wloop"), "head"),
        P(),
        P("wloop", "head"),
        P("wloop", "head"),
        P("wloop", "head"),
        P(("grp", "wloop"), None, "head"),
        P(("grp", "wloop"), None, "head"),
        P(("grp", "wloop")),
        P(("grp", "wloop")),
    )
    return jax.shard_map(
        local,
        mesh=mesh,
        in_specs=placed,
        out_specs=(
            P(("grp", "wloop"), "head"),
            P(("grp", "wloop"), "head"),
            P(("grp", "wloop"), "head"),
        ),
        check_vma=False,
    )
```

```python
import functools

import jax
import jax.numpy as jnp
from jax import lax
from jax.experimental import pallas as pl
from jax.experimental.pallas import tpu as pltpu
from jax.sharding import PartitionSpec as P

HEAD_DIM = 128


EPSILON = 1e-06
THETA = 1000000.0


def rotate(vectors, positions):
    half_dim = vectors.shape[-1] // 2
    freq_index = jnp.arange(half_dim, dtype=jnp.float32)
    frequency = jnp.power(jnp.float32(THETA), freq_index * (-2.0 / vectors.shape[-1]))
    angles = positions[..., None] * frequency
    cosine = jnp.cos(angles)
    sine_part = jnp.sin(angles)
    lower_half = vectors[..., :half_dim]
    upper_half = vectors[..., half_dim:]
    return jnp.concatenate(
        [
            lower_half * cosine - upper_half * sine_part,
            upper_half * cosine + lower_half * sine_part,
        ],
        axis=-1,
    )


def project_rows(normed, weight_rows):
    return jnp.dot(normed, weight_rows, preferred_element_type=jnp.float32)


def attend_all(rotated, new_keys, new_values, old_keys, old_values, turn_len, cache_len):
    session_count, turn_size, kv_local, head_dim = new_keys.shape
    head_local = rotated.shape[2]
    group_size = head_local // kv_local
    cache_size = old_keys.shape[1]
    factor = head_dim ** (-0.5)
    grouped = rotated.reshape(session_count, turn_size, kv_local, group_size, head_dim)
    far_scores = (
        jnp.einsum("stkgd,slkd->skgtl", grouped, old_keys, preferred_element_type=jnp.float32)
        * factor
    )
    near_scores = (
        jnp.einsum("stkgd,sukd->skgtu", grouped, new_keys, preferred_element_type=jnp.float32)
        * factor
    )
    slot_index = jnp.arange(cache_size, dtype=jnp.int32)
    turn_index = jnp.arange(turn_size, dtype=jnp.int32)
    slot_live = slot_index[None, :] < cache_len[:, None]
    far_scores = jnp.where(slot_live[:, None, None, None, :], far_scores, -jnp.inf)
    near_scores = jnp.where(turn_index[None, :] <= turn_index[:, None], near_scores, -jnp.inf)
    row_max = jnp.maximum(jnp.max(far_scores, axis=-1), jnp.max(near_scores, axis=-1))[..., None]
    far_exp = jnp.exp(far_scores - row_max)
    near_exp = jnp.exp(near_scores - row_max)
    totals = jnp.sum(far_exp, axis=-1, keepdims=True) + jnp.sum(near_exp, axis=-1, keepdims=True)
    far_weights = (far_exp / totals).astype(jnp.bfloat16)
    near_weights = (near_exp / totals).astype(jnp.bfloat16)
    mixed = jnp.einsum(
        "skgtl,slkd->stkgd", far_weights, old_values, preferred_element_type=jnp.float32
    )
    mixed = mixed + jnp.einsum(
        "skgtu,sukd->stkgd", near_weights, new_values, preferred_element_type=jnp.float32
    )
    live_rows = turn_index[None, :] < turn_len[:, None]
    mixed = jnp.where(live_rows[:, :, None, None, None], mixed, 0.0)
    return mixed.reshape(session_count * turn_size, head_local * head_dim).astype(jnp.bfloat16)


def local_gather(tokens, norm_gain, w_query, w_key, w_value, cache_key, cache_value, turn_len, cache_len):
    gathered = lax.all_gather(tokens, "head", axis=1, tiled=True)
    widened = gathered.astype(jnp.float32)
    inverse_rms = lax.rsqrt(jnp.mean(widened * widened, axis=1, keepdims=True) + EPSILON)
    normed = (widened * inverse_rms * norm_gain).astype(jnp.bfloat16)
    row_count = normed.shape[0]
    query_width = w_query.shape[1]
    pair_width = w_key.shape[1]
    queries = project_rows(normed, lax.all_gather(w_query, "wloop", axis=0, tiled=True))
    keys_raw = project_rows(normed, lax.all_gather(w_key, "wloop", axis=0, tiled=True))
    values_raw = project_rows(normed, lax.all_gather(w_value, "wloop", axis=0, tiled=True))
    session_count = turn_len.shape[0]
    turn_size = row_count // session_count
    head_local = query_width // HEAD_DIM
    kv_local = pair_width // HEAD_DIM
    turn_index = jnp.arange(turn_size, dtype=jnp.int32)
    positions = (cache_len[:, None] + turn_index[None, :]).astype(jnp.float32)[:, :, None]
    live_rows = turn_index[None, :] < turn_len[:, None]
    rotated = rotate(
        queries.reshape(session_count, turn_size, head_local, HEAD_DIM), positions
    ).astype(jnp.bfloat16)
    new_keys = jnp.where(
        live_rows[:, :, None, None],
        rotate(keys_raw.reshape(session_count, turn_size, kv_local, HEAD_DIM), positions),
        0.0,
    ).astype(jnp.bfloat16)
    new_values = jnp.where(
        live_rows[:, :, None, None],
        values_raw.reshape(session_count, turn_size, kv_local, HEAD_DIM),
        0.0,
    ).astype(jnp.bfloat16)
    old_keys = cache_key.reshape(session_count, cache_key.shape[1], kv_local, HEAD_DIM)
    old_values = cache_value.reshape(session_count, cache_value.shape[1], kv_local, HEAD_DIM)
    attended = attend_all(rotated, new_keys, new_values, old_keys, old_values, turn_len, cache_len)
    return (
        attended,
        new_keys.reshape(row_count, pair_width),
        new_values.reshape(row_count, pair_width),
    )


def column_of(row):
    lanes = row.shape[1]
    return jnp.transpose(jnp.broadcast_to(row, (lanes, lanes)))[:, :1]


def row_of(column):
    lanes = column.shape[0]
    return jnp.transpose(jnp.broadcast_to(column, (lanes, lanes)))[:8, :]


def move_kernel(
    width,
    tokens_ref,
    gain_ref,
    out_ref,
    stage,
    mine,
    sums,
    piece_send,
    piece_recv,
    self_sem,
    sums_send,
    sums_recv,
    pair_send,
    pair_recv,
    cross_send,
    cross_recv,
    pass_send,
    pass_recv,
    own_sem,
):
    ways, rows = stage.shape[0], stage.shape[1]
    w_at, h_at = lax.axis_index("wloop"), lax.axis_index("head")

    def device(w, h):
        return {"wloop": w, "head": h}

    barrier = pltpu.get_barrier_semaphore()
    for dw in range(ways):
        for dh in range(ways):
            if dw or dh:
                pl.semaphore_signal(
                    barrier,
                    inc=1,
                    device_id=device(lax.rem(w_at + dw, ways), lax.rem(h_at + dh, ways)),
                    device_id_type=pl.DeviceIdType.MESH,
                )
    pl.semaphore_wait(barrier, ways * ways - 1)

    def remote(source, target, send, recv, w, h):
        return pltpu.make_async_remote_copy(
            src_ref=source,
            dst_ref=target,
            send_sem=send,
            recv_sem=recv,
            device_id=device(w, h),
            device_id_type=pl.DeviceIdType.MESH,
        )

    pieces = []
    for j in range(ways):
        to = lax.rem(w_at + j, ways)
        source = tokens_ref.at[pl.ds(pl.multiple_of(to * rows, rows), rows), :]
        pieces.append(
            remote(source, stage.at[w_at], piece_send.at[j], piece_recv.at[j], h_at, to)
        )
    kept = pltpu.make_async_copy(
        tokens_ref.at[pl.ds(pl.multiple_of(w_at * rows, rows), rows), :],
        stage.at[w_at],
        self_sem,
    )

    @pl.when(w_at != h_at)
    def _():
        pieces[0].start()

    @pl.when(w_at == h_at)
    def _():
        kept.start()

    for j in range(1, ways):
        pieces[j].start()

    sibling = h_at + 1 - 2 * lax.rem(h_at, 2)
    partner = lax.rem(h_at + ways // 2, ways)

    def block_of(j):
        return lax.rem(h_at + ways - j, ways)

    exchanges = [
        [
            remote(
                sums.at[j, w_at],
                sums.at[j, w_at],
                sums_send.at[j, k - 1],
                sums_recv.at[j, k - 1],
                lax.rem(w_at + k, ways),
                h_at,
            )
            for k in range(1, ways)
        ]
        for j in range(ways)
    ]
    sends = []
    for j in range(ways):
        block = block_of(j)
        sends.append(
            (
                pltpu.make_async_copy(mine.at[block], out_ref.at[block, h_at], own_sem.at[j]),
                remote(
                    mine.at[block],
                    out_ref.at[block, h_at],
                    cross_send.at[j],
                    cross_recv.at[j],
                    w_at,
                    partner,
                ),
                remote(
                    mine.at[block],
                    out_ref.at[block, h_at],
                    pair_send.at[j],
                    pair_recv.at[j],
                    w_at,
                    sibling,
                ),
            )
        )

    def take_in(j):
        if j == 0:

            @pl.when(w_at != h_at)
            def _():
                pieces[0].wait_recv()

            @pl.when(w_at == h_at)
            def _():
                kept.wait()
        else:
            pieces[j].wait_recv()
        total = None
        held = stage[block_of(j)].astype(jnp.float32)
        total = jnp.sum(held * held, axis=1, keepdims=True)
        sums[j, w_at] = row_of(total)
        for exchange in exchanges[j]:
            exchange.start()

    def give_out(j):
        for exchange in exchanges[j]:
            exchange.wait_recv()
        total = sums[j, 0]
        for w in range(1, ways):
            total = total + sums[j, w]
        inverse = column_of(lax.rsqrt(total[:1] / width + EPSILON))
        block = block_of(j)
        held = stage[block].astype(jnp.float32)
        mine[block] = (held * inverse * gain_ref[...]).astype(jnp.bfloat16)
        for copy in reversed(sends[j]):
            copy.start()

    take_in(0)
    for j in range(1, ways):
        take_in(j)
        give_out(j - 1)
    give_out(ways - 1)

    passes = []
    for j in range(ways):
        block = lax.rem(partner + ways - j, ways)
        sends[j][1].wait_recv()
        passed = remote(
            out_ref.at[block, partner],
            out_ref.at[block, partner],
            pass_send.at[j],
            pass_recv.at[j],
            w_at,
            sibling,
        )
        passed.start()
        passes.append(passed)
    for j in range(ways):
        sends[j][0].wait()
        sends[j][1].wait_send()
        sends[j][2].wait()
        passes[j].wait()
        for exchange in exchanges[j]:
            exchange.wait_send()
        if j:
            pieces[j].wait_send()

    @pl.when(w_at != h_at)
    def _():
        pieces[0].wait_send()


def moved_normed(tokens, gain, width, ways):
    row_count, depth = tokens.shape
    rows = row_count // ways
    pair = pltpu.SemaphoreType.DMA((ways,))
    grid = pltpu.SemaphoreType.DMA((ways, ways - 1))
    moved = pl.pallas_call(
        functools.partial(move_kernel, width),
        out_shape=jax.ShapeDtypeStruct((ways, ways, rows, depth), jnp.bfloat16),
        in_specs=[
            pl.BlockSpec(memory_space=pl.ANY),
            pl.BlockSpec(memory_space=pltpu.VMEM),
        ],
        out_specs=pl.BlockSpec(memory_space=pl.ANY),
        scratch_shapes=[
            pltpu.VMEM((ways, rows, depth), jnp.bfloat16),
            pltpu.VMEM((ways, rows, depth), jnp.bfloat16),
            pltpu.VMEM((ways, ways, 8, rows), jnp.float32),
            pair,
            pair,
            pltpu.SemaphoreType.DMA,
            grid,
            grid,
            pair,
            pair,
            pair,
            pair,
            pair,
            pair,
            pair,
        ],
        compiler_params=pltpu.CompilerParams(
            collective_id=0, has_side_effects=True, vmem_limit_bytes=24 * 1024 * 1024
        ),
    )(tokens, gain.reshape(1, depth))
    return moved.reshape(ways, row_count, depth)


def attend_kernel(
    group_size, turn_len_ref, cache_len_ref, q_ref, kv_ref, cos_ref, sin_ref, old_k_ref, old_v_ref,
    out_ref, new_k_ref, new_v_ref,
):
    at = pl.program_id(0)
    turn_size, head_dim = cos_ref.shape
    cache_size = old_k_ref.shape[1]
    cosine, sine = cos_ref[...], sin_ref[...]

    def turned(v):
        return v * cosine + pltpu.roll(v, head_dim // 2, 1) * sine

    live = lax.broadcasted_iota(jnp.int32, (turn_size, head_dim), 0) < turn_len_ref[at]
    new_k = jnp.where(live, turned(kv_ref[:, :head_dim]), 0.0).astype(jnp.bfloat16)
    new_v = jnp.where(live, kv_ref[:, head_dim:], 0.0).astype(jnp.bfloat16)
    new_k_ref[...] = new_k
    new_v_ref[...] = new_v
    old_k, old_v = old_k_ref[0], old_v_ref[0]
    slot_live = lax.broadcasted_iota(jnp.int32, (1, cache_size), 1) < cache_len_ref[at]
    bias = jnp.where(slot_live, 0.0, -jnp.inf)
    causal = lax.broadcasted_iota(jnp.int32, (turn_size, turn_size), 1) <= (
        lax.broadcasted_iota(jnp.int32, (turn_size, turn_size), 0)
    )
    factor = head_dim ** (-0.5)
    contract = (((1,), (1,)), ((), ()))
    for head in range(group_size):
        cols = slice(head * head_dim, (head + 1) * head_dim)
        query = turned(q_ref[:, cols]).astype(jnp.bfloat16)
        far = lax.dot_general(query, old_k, contract, preferred_element_type=jnp.float32)
        near = lax.dot_general(query, new_k, contract, preferred_element_type=jnp.float32)
        far = far * factor + bias
        near = jnp.where(causal, near * factor, -jnp.inf)
        top = jnp.maximum(
            jnp.max(far, axis=1, keepdims=True), jnp.max(near, axis=1, keepdims=True)
        )
        far = jnp.exp(far - top)
        near = jnp.exp(near - top)
        total = jnp.sum(far, axis=1, keepdims=True) + jnp.sum(near, axis=1, keepdims=True)
        scale = 1.0 / total
        mixed = jnp.dot(
            (far * scale).astype(jnp.bfloat16), old_v, preferred_element_type=jnp.float32
        ) + jnp.dot((near * scale).astype(jnp.bfloat16), new_v, preferred_element_type=jnp.float32)
        out_ref[:, cols] = jnp.where(live, mixed, 0.0).astype(jnp.bfloat16)


def attend_part(summed, cosine, sine, cache_key, cache_value, turn_len, cache_len, kv):
    row_count, width = summed.shape
    sessions, cache_size, _ = cache_key.shape
    turn_size = row_count // sessions
    q_cols = width - 2 * HEAD_DIM
    smem = pl.BlockSpec(memory_space=pltpu.SMEM)
    rows = lambda cols, at=0: pl.BlockSpec((turn_size, cols), lambda s: (s, at))
    cached = pl.BlockSpec((1, cache_size, HEAD_DIM), lambda s: (s, 0, kv))
    bf16 = lambda cols: jax.ShapeDtypeStruct((row_count, cols), jnp.bfloat16)
    work = row_count * q_cols * (cache_size + turn_size)
    return pl.pallas_call(
        functools.partial(attend_kernel, q_cols // HEAD_DIM),
        grid=(sessions,),
        out_shape=(bf16(q_cols), bf16(HEAD_DIM), bf16(HEAD_DIM)),
        in_specs=[
            smem,
            smem,
            rows(q_cols),
            rows(2 * HEAD_DIM, q_cols // (2 * HEAD_DIM)),
            rows(HEAD_DIM),
            rows(HEAD_DIM),
            cached,
            cached,
        ],
        out_specs=(rows(q_cols), rows(HEAD_DIM), rows(HEAD_DIM)),
        compiler_params=pltpu.CompilerParams(vmem_limit_bytes=32 * 1024 * 1024),
        cost_estimate=pl.CostEstimate(
            flops=16 * work, bytes_accessed=10**7, transcendentals=work // HEAD_DIM
        ),
    )(turn_len, cache_len, summed, summed, cosine, sine, cache_key, cache_value)


def reduce_over_line(partials, ways, after):
    w_at = lax.axis_index("wloop")

    def pick(index):
        return lax.dynamic_index_in_dim(
            partials, jnp.clip(index, 0, ways - 1), 0, keepdims=False
        )

    rising = None
    falling = None
    middle = None
    for step in range(1, ways):
        up = pick(w_at + ways - step)
        down = pick(w_at - ways + step)
        if rising is not None:
            up = up + rising.astype(jnp.float32)
            down = down + falling.astype(jnp.float32)
        up, down = up.astype(jnp.bfloat16), down.astype(jnp.bfloat16)
        if step == 1 and after is not None:
            up, down, _ = lax.optimization_barrier((up, down, after))
        if step == ways - 1:
            middle = up[:8], down[:8]
        rising = lax.ppermute(up, "wloop", [(w, w + 1) for w in range(step)])
        falling = lax.ppermute(
            down, "wloop", [(ways - 1 - w, ways - 2 - w) for w in range(step)]
        )
    summed = pick(w_at) + rising.astype(jnp.float32) + falling.astype(jnp.float32)
    return summed, middle


def local_reduce(
    tokens, norm_gain, w_query, w_key, w_value, cache_key, cache_value, turn_len, cache_len
):
    ways = lax.axis_size("wloop")
    row_count = tokens.shape[0]
    depth = w_query.shape[0]
    width = norm_gain.shape[0]
    kv_local = w_key.shape[1] // HEAD_DIM
    q_cols = w_query.shape[1] // kv_local
    turn_size = row_count // turn_len.shape[0]
    w_at = lax.axis_index("wloop")

    gain = lax.dynamic_slice_in_dim(norm_gain, w_at * depth, depth, 0)
    normed = moved_normed(tokens, gain, width, ways)

    half_dim = HEAD_DIM // 2
    freq_index = jnp.arange(half_dim, dtype=jnp.float32)
    frequency = jnp.power(jnp.float32(THETA), freq_index * (-2.0 / HEAD_DIM))
    turn_index = jnp.arange(turn_size, dtype=jnp.int32)
    positions = (cache_len[:, None] + turn_index[None, :]).astype(jnp.float32)
    angles = positions.reshape(row_count, 1) * frequency
    cosine, sine = jnp.cos(angles), jnp.sin(angles)
    cosine = jnp.concatenate([cosine, cosine], axis=1)
    sine = jnp.concatenate([-sine, sine], axis=1)

    outs = []
    after = None
    for kv in range(kv_local):
        weights = jnp.concatenate(
            [
                w_query[:, kv * q_cols : (kv + 1) * q_cols],
                w_key[:, kv * HEAD_DIM : (kv + 1) * HEAD_DIM],
                w_value[:, kv * HEAD_DIM : (kv + 1) * HEAD_DIM],
            ],
            axis=1,
        )
        partials = jnp.einsum("brd,dn->brn", normed, weights, preferred_element_type=jnp.float32)
        summed, after = reduce_over_line(partials, ways, after)
        outs.append(
            attend_part(summed, cosine, sine, cache_key, cache_value, turn_len, cache_len, kv)
        )
    return tuple(jnp.concatenate(arrays, axis=1) for arrays in zip(*outs))


def local(*args):
    tokens, norm_gain = args[0], args[1]
    w_ways, h_ways = lax.axis_size("wloop"), lax.axis_size("head")
    if w_ways == h_ways == 4 and tokens.shape[0] == w_ways * HEAD_DIM:
        if w_ways * tokens.shape[0] < norm_gain.shape[0]:
            return local_reduce(*args)
    return local_gather(*args)


def solution(mesh):
    placed = (
        P(("grp", "wloop"), "head"),
        P(),
        P("wloop", "head"),
        P("wloop", "head"),
        P("wloop", "head"),
        P(("grp", "wloop"), None, "head"),
        P(("grp", "wloop"), None, "head"),
        P(("grp", "wloop")),
        P(("grp", "wloop")),
    )
    return jax.shard_map(
        local,
        mesh=mesh,
        in_specs=placed,
        out_specs=(
            P(("grp", "wloop"), "head"),
            P(("grp", "wloop"), "head"),
            P(("grp", "wloop"), "head"),
        ),
        check_vma=False,
    )
```

```python
import functools

import jax
import jax.numpy as jnp
from jax import lax
from jax.experimental import pallas as pl
from jax.experimental.pallas import tpu as pltpu
from jax.sharding import PartitionSpec as P

HEAD_DIM = 128


EPSILON = 1e-06
THETA = 1000000.0


def rotate(vectors, positions):
    half_dim = vectors.shape[-1] // 2
    freq_index = jnp.arange(half_dim, dtype=jnp.float32)
    frequency = jnp.power(jnp.float32(THETA), freq_index * (-2.0 / vectors.shape[-1]))
    angles = positions[..., None] * frequency
    cosine = jnp.cos(angles)
    sine_part = jnp.sin(angles)
    lower_half = vectors[..., :half_dim]
    upper_half = vectors[..., half_dim:]
    return jnp.concatenate(
        [
            lower_half * cosine - upper_half * sine_part,
            upper_half * cosine + lower_half * sine_part,
        ],
        axis=-1,
    )


def project_rows(normed, weight_rows):
    return jnp.dot(normed, weight_rows, preferred_element_type=jnp.float32)


def attend_all(rotated, new_keys, new_values, old_keys, old_values, turn_len, cache_len):
    session_count, turn_size, kv_local, head_dim = new_keys.shape
    head_local = rotated.shape[2]
    group_size = head_local // kv_local
    cache_size = old_keys.shape[1]
    factor = head_dim ** (-0.5)
    grouped = rotated.reshape(session_count, turn_size, kv_local, group_size, head_dim)
    far_scores = (
        jnp.einsum("stkgd,slkd->skgtl", grouped, old_keys, preferred_element_type=jnp.float32)
        * factor
    )
    near_scores = (
        jnp.einsum("stkgd,sukd->skgtu", grouped, new_keys, preferred_element_type=jnp.float32)
        * factor
    )
    slot_index = jnp.arange(cache_size, dtype=jnp.int32)
    turn_index = jnp.arange(turn_size, dtype=jnp.int32)
    slot_live = slot_index[None, :] < cache_len[:, None]
    far_scores = jnp.where(slot_live[:, None, None, None, :], far_scores, -jnp.inf)
    near_scores = jnp.where(turn_index[None, :] <= turn_index[:, None], near_scores, -jnp.inf)
    row_max = jnp.maximum(jnp.max(far_scores, axis=-1), jnp.max(near_scores, axis=-1))[..., None]
    far_exp = jnp.exp(far_scores - row_max)
    near_exp = jnp.exp(near_scores - row_max)
    totals = jnp.sum(far_exp, axis=-1, keepdims=True) + jnp.sum(near_exp, axis=-1, keepdims=True)
    far_weights = (far_exp / totals).astype(jnp.bfloat16)
    near_weights = (near_exp / totals).astype(jnp.bfloat16)
    mixed = jnp.einsum(
        "skgtl,slkd->stkgd", far_weights, old_values, preferred_element_type=jnp.float32
    )
    mixed = mixed + jnp.einsum(
        "skgtu,sukd->stkgd", near_weights, new_values, preferred_element_type=jnp.float32
    )
    live_rows = turn_index[None, :] < turn_len[:, None]
    mixed = jnp.where(live_rows[:, :, None, None, None], mixed, 0.0)
    return mixed.reshape(session_count * turn_size, head_local * head_dim).astype(jnp.bfloat16)


def local_gather(tokens, norm_gain, w_query, w_key, w_value, cache_key, cache_value, turn_len, cache_len):
    gathered = lax.all_gather(tokens, "head", axis=1, tiled=True)
    widened = gathered.astype(jnp.float32)
    inverse_rms = lax.rsqrt(jnp.mean(widened * widened, axis=1, keepdims=True) + EPSILON)
    normed = (widened * inverse_rms * norm_gain).astype(jnp.bfloat16)
    row_count = normed.shape[0]
    query_width = w_query.shape[1]
    pair_width = w_key.shape[1]
    queries = project_rows(normed, lax.all_gather(w_query, "wloop", axis=0, tiled=True))
    keys_raw = project_rows(normed, lax.all_gather(w_key, "wloop", axis=0, tiled=True))
    values_raw = project_rows(normed, lax.all_gather(w_value, "wloop", axis=0, tiled=True))
    session_count = turn_len.shape[0]
    turn_size = row_count // session_count
    head_local = query_width // HEAD_DIM
    kv_local = pair_width // HEAD_DIM
    turn_index = jnp.arange(turn_size, dtype=jnp.int32)
    positions = (cache_len[:, None] + turn_index[None, :]).astype(jnp.float32)[:, :, None]
    live_rows = turn_index[None, :] < turn_len[:, None]
    rotated = rotate(
        queries.reshape(session_count, turn_size, head_local, HEAD_DIM), positions
    ).astype(jnp.bfloat16)
    new_keys = jnp.where(
        live_rows[:, :, None, None],
        rotate(keys_raw.reshape(session_count, turn_size, kv_local, HEAD_DIM), positions),
        0.0,
    ).astype(jnp.bfloat16)
    new_values = jnp.where(
        live_rows[:, :, None, None],
        values_raw.reshape(session_count, turn_size, kv_local, HEAD_DIM),
        0.0,
    ).astype(jnp.bfloat16)
    old_keys = cache_key.reshape(session_count, cache_key.shape[1], kv_local, HEAD_DIM)
    old_values = cache_value.reshape(session_count, cache_value.shape[1], kv_local, HEAD_DIM)
    attended = attend_all(rotated, new_keys, new_values, old_keys, old_values, turn_len, cache_len)
    return (
        attended,
        new_keys.reshape(row_count, pair_width),
        new_values.reshape(row_count, pair_width),
    )


def column_of(row):
    lanes = row.shape[1]
    return jnp.transpose(jnp.broadcast_to(row, (lanes, lanes)))[:, :1]


def row_of(column):
    lanes = column.shape[0]
    return jnp.transpose(jnp.broadcast_to(column, (lanes, lanes)))[:8, :]


def move_kernel(
    width,
    tokens_ref,
    gain_ref,
    out_ref,
    stage,
    relay,
    mine,
    sums,
    piece_send,
    piece_recv,
    relay_send,
    relay_recv,
    self_sem,
    sums_send,
    sums_recv,
    pair_send,
    pair_recv,
    cross_send,
    cross_recv,
    pass_send,
    pass_recv,
    own_sem,
):
    ways, rows = stage.shape[0], stage.shape[1]
    w_at, h_at = lax.axis_index("wloop"), lax.axis_index("head")

    def device(w, h):
        return {"wloop": w, "head": h}

    barrier = pltpu.get_barrier_semaphore()
    for dw in range(ways):
        for dh in range(ways):
            if dw or dh:
                pl.semaphore_signal(
                    barrier,
                    inc=1,
                    device_id=device(lax.rem(w_at + dw, ways), lax.rem(h_at + dh, ways)),
                    device_id_type=pl.DeviceIdType.MESH,
                )
    pl.semaphore_wait(barrier, ways * ways - 1)

    def remote(source, target, send, recv, w, h):
        return pltpu.make_async_remote_copy(
            src_ref=source,
            dst_ref=target,
            send_sem=send,
            recv_sem=recv,
            device_id=device(w, h),
            device_id_type=pl.DeviceIdType.MESH,
        )

    sibling = h_at + 1 - 2 * lax.rem(h_at, 2)
    partner = lax.rem(h_at + ways // 2, ways)
    across = lax.rem(sibling + ways // 2, ways)

    def rows_for(h):
        return tokens_ref.at[pl.ds(pl.multiple_of(h * rows, rows), rows), :]

    def to_stage(source, at, w, h):
        return remote(source, stage.at[w_at], piece_send.at[at], piece_recv.at[w_at], w, h)

    crossing = [
        remote(rows_for(h), relay.at[at], relay_send.at[at], relay_recv.at[at], w_at, partner)
        for at, h in enumerate((across, partner))
    ]
    for copy in crossing:
        copy.start()
    beside = to_stage(rows_for(sibling), 0, h_at, sibling)
    beside.start()
    straight = to_stage(rows_for(h_at), 1, h_at, h_at)
    kept = pltpu.make_async_copy(rows_for(h_at), stage.at[w_at], self_sem.at[0])
    relayed_beside = to_stage(relay.at[0], 2, partner, sibling)
    relayed = to_stage(relay.at[1], 3, partner, h_at)
    relay_kept = pltpu.make_async_copy(relay.at[1], stage.at[w_at], self_sem.at[1])

    @pl.when(w_at != h_at)
    def _():
        straight.start()

    @pl.when(w_at == h_at)
    def _():
        kept.start()

    crossing[0].wait_recv()
    relayed_beside.start()
    crossing[1].wait_recv()

    @pl.when(w_at != partner)
    def _():
        relayed.start()

    @pl.when(w_at == partner)
    def _():
        relay_kept.start()

    def arrival(block):
        return pltpu.make_async_remote_copy(
            src_ref=stage.at[block],
            dst_ref=stage.at[block],
            send_sem=piece_send.at[0],
            recv_sem=piece_recv.at[block],
            device_id=device(w_at, sibling),
            device_id_type=pl.DeviceIdType.MESH,
        )

    def block_of(j):
        return lax.rem(h_at + ways - j, ways)

    exchanges = [
        [
            remote(
                sums.at[j, w_at],
                sums.at[j, w_at],
                sums_send.at[j, k - 1],
                sums_recv.at[j, k - 1],
                lax.rem(w_at + k, ways),
                h_at,
            )
            for k in range(1, ways)
        ]
        for j in range(ways)
    ]
    sends = []
    for j in range(ways):
        block = block_of(j)
        sends.append(
            (
                pltpu.make_async_copy(mine.at[block], out_ref.at[block, h_at], own_sem.at[j]),
                remote(
                    mine.at[block],
                    out_ref.at[block, h_at],
                    cross_send.at[j],
                    cross_recv.at[j],
                    w_at,
                    partner,
                ),
                remote(
                    mine.at[block],
                    out_ref.at[block, h_at],
                    pair_send.at[j],
                    pair_recv.at[j],
                    w_at,
                    sibling,
                ),
            )
        )

    def take_in(j):
        block = block_of(j)
        own = jnp.logical_and(block == w_at, lax.rem(h_at, ways // 2) == lax.rem(w_at, ways // 2))

        @pl.when(jnp.logical_not(own))
        def _():
            arrival(block).wait_recv()

        @pl.when(jnp.logical_and(own, w_at == h_at))
        def _():
            kept.wait()

        @pl.when(jnp.logical_and(own, w_at != h_at))
        def _():
            relay_kept.wait()

        held = stage[block].astype(jnp.float32)
        total = jnp.sum(held * held, axis=1, keepdims=True)
        sums[j, w_at] = row_of(total)
        for exchange in exchanges[j]:
            exchange.start()

    def give_out(j):
        for exchange in exchanges[j]:
            exchange.wait_recv()
        total = sums[j, 0]
        for w in range(1, ways):
            total = total + sums[j, w]
        inverse = column_of(lax.rsqrt(total[:1] / width + EPSILON))
        block = block_of(j)
        held = stage[block].astype(jnp.float32)
        mine[block] = (held * inverse * gain_ref[...]).astype(jnp.bfloat16)
        for copy in reversed(sends[j]):
            copy.start()

    take_in(0)
    for j in range(1, ways):
        take_in(j)
        give_out(j - 1)
    give_out(ways - 1)

    passes = []
    for j in range(ways):
        block = lax.rem(partner + ways - j, ways)
        sends[j][1].wait_recv()
        passed = remote(
            out_ref.at[block, partner],
            out_ref.at[block, partner],
            pass_send.at[j],
            pass_recv.at[j],
            w_at,
            sibling,
        )
        passed.start()
        passes.append(passed)
    for j in range(ways):
        sends[j][0].wait()
        sends[j][1].wait_send()
        sends[j][2].wait()
        passes[j].wait()
        for exchange in exchanges[j]:
            exchange.wait_send()
    beside.wait_send()
    relayed_beside.wait_send()
    for copy in crossing:
        copy.wait_send()

    @pl.when(w_at != h_at)
    def _():
        straight.wait_send()

    @pl.when(w_at != partner)
    def _():
        relayed.wait_send()


def moved_normed(tokens, gain, width, ways):
    row_count, depth = tokens.shape
    rows = row_count // ways
    pair = pltpu.SemaphoreType.DMA((ways,))
    grid = pltpu.SemaphoreType.DMA((ways, ways - 1))
    moved = pl.pallas_call(
        functools.partial(move_kernel, width),
        out_shape=jax.ShapeDtypeStruct((ways, ways, rows, depth), jnp.bfloat16),
        in_specs=[
            pl.BlockSpec(memory_space=pl.ANY),
            pl.BlockSpec(memory_space=pltpu.VMEM),
        ],
        out_specs=pl.BlockSpec(memory_space=pl.ANY),
        scratch_shapes=[
            pltpu.VMEM((ways, rows, depth), jnp.bfloat16),
            pltpu.VMEM((2, rows, depth), jnp.bfloat16),
            pltpu.VMEM((ways, rows, depth), jnp.bfloat16),
            pltpu.VMEM((ways, ways, 8, rows), jnp.float32),
            pair,
            pair,
            pltpu.SemaphoreType.DMA((2,)),
            pltpu.SemaphoreType.DMA((2,)),
            pltpu.SemaphoreType.DMA((2,)),
            grid,
            grid,
            pair,
            pair,
            pair,
            pair,
            pair,
            pair,
            pair,
        ],
        compiler_params=pltpu.CompilerParams(
            collective_id=0, has_side_effects=True, vmem_limit_bytes=24 * 1024 * 1024
        ),
    )(tokens, gain.reshape(1, depth))
    return moved.reshape(ways, row_count, depth)


def attend_kernel(
    group_size, turn_len_ref, cache_len_ref, q_ref, kv_ref, cos_ref, sin_ref, old_k_ref, old_v_ref,
    out_ref, new_k_ref, new_v_ref,
):
    at = pl.program_id(0)
    turn_size, head_dim = cos_ref.shape
    cache_size = old_k_ref.shape[1]
    cosine, sine = cos_ref[...], sin_ref[...]

    def turned(v):
        return v * cosine + pltpu.roll(v, head_dim // 2, 1) * sine

    live = lax.broadcasted_iota(jnp.int32, (turn_size, head_dim), 0) < turn_len_ref[at]
    new_k = jnp.where(live, turned(kv_ref[:, :head_dim]), 0.0).astype(jnp.bfloat16)
    new_v = jnp.where(live, kv_ref[:, head_dim:], 0.0).astype(jnp.bfloat16)
    new_k_ref[...] = new_k
    new_v_ref[...] = new_v
    old_k, old_v = old_k_ref[0], old_v_ref[0]
    slot_live = lax.broadcasted_iota(jnp.int32, (1, cache_size), 1) < cache_len_ref[at]
    bias = jnp.where(slot_live, 0.0, -jnp.inf)
    stack = 2 if group_size % 2 == 0 else 1
    causal = lax.broadcasted_iota(jnp.int32, (turn_size, turn_size), 1) <= (
        lax.broadcasted_iota(jnp.int32, (turn_size, turn_size), 0)
    )
    near_bias = jnp.concatenate([jnp.where(causal, 0.0, -jnp.inf)] * stack, axis=0)
    factor = head_dim ** (-0.5)
    contract = (((1,), (1,)), ((), ()))
    for first in range(0, group_size, stack):
        cols = [slice(h * head_dim, (h + 1) * head_dim) for h in range(first, first + stack)]
        query = jnp.concatenate([turned(q_ref[:, c]) for c in cols], axis=0).astype(jnp.bfloat16)
        far = lax.dot_general(query, old_k, contract, preferred_element_type=jnp.float32)
        near = lax.dot_general(query, new_k, contract, preferred_element_type=jnp.float32)
        far = far * factor + bias
        near = near * factor + near_bias
        top = jnp.maximum(
            jnp.max(far, axis=1, keepdims=True), jnp.max(near, axis=1, keepdims=True)
        )
        far = jnp.exp(far - top)
        near = jnp.exp(near - top)
        total = jnp.sum(far, axis=1, keepdims=True) + jnp.sum(near, axis=1, keepdims=True)
        mixed = jnp.dot(
            far.astype(jnp.bfloat16), old_v, preferred_element_type=jnp.float32
        ) + jnp.dot(near.astype(jnp.bfloat16), new_v, preferred_element_type=jnp.float32)
        mixed = mixed * (1.0 / total)
        for at, c in enumerate(cols):
            block = mixed[at * turn_size : (at + 1) * turn_size]
            out_ref[:, c] = jnp.where(live, block, 0.0).astype(jnp.bfloat16)


def attend_part(summed, cosine, sine, cache_key, cache_value, turn_len, cache_len, kv):
    row_count, width = summed.shape
    sessions, cache_size, _ = cache_key.shape
    turn_size = row_count // sessions
    q_cols = width - 2 * HEAD_DIM
    smem = pl.BlockSpec(memory_space=pltpu.SMEM)
    rows = lambda cols, at=0: pl.BlockSpec((turn_size, cols), lambda s: (s, at))
    cached = pl.BlockSpec((1, cache_size, HEAD_DIM), lambda s: (s, 0, kv))
    bf16 = lambda cols: jax.ShapeDtypeStruct((row_count, cols), jnp.bfloat16)
    work = row_count * q_cols * (cache_size + turn_size)
    return pl.pallas_call(
        functools.partial(attend_kernel, q_cols // HEAD_DIM),
        grid=(sessions,),
        out_shape=(bf16(q_cols), bf16(HEAD_DIM), bf16(HEAD_DIM)),
        in_specs=[
            smem,
            smem,
            rows(q_cols),
            rows(2 * HEAD_DIM, q_cols // (2 * HEAD_DIM)),
            rows(HEAD_DIM),
            rows(HEAD_DIM),
            cached,
            cached,
        ],
        out_specs=(rows(q_cols), rows(HEAD_DIM), rows(HEAD_DIM)),
        compiler_params=pltpu.CompilerParams(vmem_limit_bytes=32 * 1024 * 1024),
        cost_estimate=pl.CostEstimate(
            flops=16 * work, bytes_accessed=10**7, transcendentals=work // HEAD_DIM
        ),
    )(turn_len, cache_len, summed, summed, cosine, sine, cache_key, cache_value)


def zero_after(array):
    first = array[(0,) * array.ndim]
    return (first > jnp.inf).astype(jnp.int32)


def reduce_over_line(partials, ways, after):
    w_at = lax.axis_index("wloop")

    def pick(index):
        return lax.dynamic_index_in_dim(
            partials, jnp.clip(index, 0, ways - 1), 0, keepdims=False
        )

    rising = None
    falling = None
    middle = None
    for step in range(1, ways):
        hold = zero_after(after) if step == 1 and after is not None else 0
        up = pick(w_at + ways - step + hold)
        down = pick(w_at - ways + step + hold)
        if rising is not None:
            up = up + rising.astype(jnp.float32)
            down = down + falling.astype(jnp.float32)
            if middle is None:
                middle = rising
        up, down = up.astype(jnp.bfloat16), down.astype(jnp.bfloat16)
        rising = lax.ppermute(up, "wloop", [(w, w + 1) for w in range(step)])
        falling = lax.ppermute(
            down, "wloop", [(ways - 1 - w, ways - 2 - w) for w in range(step)]
        )
    summed = pick(w_at) + rising.astype(jnp.float32) + falling.astype(jnp.float32)
    return summed, middle


def local_reduce(
    tokens, norm_gain, w_query, w_key, w_value, cache_key, cache_value, turn_len, cache_len
):
    ways = lax.axis_size("wloop")
    row_count = tokens.shape[0]
    depth = w_query.shape[0]
    width = norm_gain.shape[0]
    kv_local = w_key.shape[1] // HEAD_DIM
    q_cols = w_query.shape[1] // kv_local
    turn_size = row_count // turn_len.shape[0]
    w_at = lax.axis_index("wloop")

    gain = lax.dynamic_slice_in_dim(norm_gain, w_at * depth, depth, 0)
    normed = moved_normed(tokens, gain, width, ways)

    half_dim = HEAD_DIM // 2
    freq_index = jnp.arange(half_dim, dtype=jnp.float32)
    frequency = jnp.power(jnp.float32(THETA), freq_index * (-2.0 / HEAD_DIM))
    turn_index = jnp.arange(turn_size, dtype=jnp.int32)
    starts = cache_len + zero_after(normed)
    positions = (starts[:, None] + turn_index[None, :]).astype(jnp.float32)
    angles = positions.reshape(row_count, 1) * frequency
    cosine, sine = jnp.cos(angles), jnp.sin(angles)
    cosine = jnp.concatenate([cosine, cosine], axis=1)
    sine = jnp.concatenate([-sine, sine], axis=1)

    outs = []
    after = None
    for kv in range(kv_local):
        weights = jnp.concatenate(
            [
                w_query[:, kv * q_cols : (kv + 1) * q_cols],
                w_key[:, kv * HEAD_DIM : (kv + 1) * HEAD_DIM],
                w_value[:, kv * HEAD_DIM : (kv + 1) * HEAD_DIM],
            ],
            axis=1,
        )
        partials = jnp.einsum("brd,dn->brn", normed, weights, preferred_element_type=jnp.float32)
        summed, after = reduce_over_line(partials, ways, after)
        outs.append(
            attend_part(summed, cosine, sine, cache_key, cache_value, turn_len, cache_len, kv)
        )
    return tuple(jnp.concatenate(arrays, axis=1) for arrays in zip(*outs))


def local(*args):
    tokens, norm_gain = args[0], args[1]
    w_ways, h_ways = lax.axis_size("wloop"), lax.axis_size("head")
    if w_ways == h_ways == 4 and tokens.shape[0] == w_ways * HEAD_DIM:
        if w_ways * tokens.shape[0] < norm_gain.shape[0]:
            return local_reduce(*args)
    return local_gather(*args)


def solution(mesh):
    placed = (
        P(("grp", "wloop"), "head"),
        P(),
        P("wloop", "head"),
        P("wloop", "head"),
        P("wloop", "head"),
        P(("grp", "wloop"), None, "head"),
        P(("grp", "wloop"), None, "head"),
        P(("grp", "wloop")),
        P(("grp", "wloop")),
    )
    return jax.shard_map(
        local,
        mesh=mesh,
        in_specs=placed,
        out_specs=(
            P(("grp", "wloop"), "head"),
            P(("grp", "wloop"), "head"),
            P(("grp", "wloop"), "head"),
        ),
        check_vma=False,
    )
```

```python
import functools

import jax
import jax.numpy as jnp
from jax import lax
from jax.experimental import pallas as pl
from jax.experimental.pallas import tpu as pltpu
from jax.sharding import PartitionSpec as P

HEAD_DIM = 128


EPSILON = 1e-06
THETA = 1000000.0


def rotate(vectors, positions):
    half_dim = vectors.shape[-1] // 2
    freq_index = jnp.arange(half_dim, dtype=jnp.float32)
    frequency = jnp.power(jnp.float32(THETA), freq_index * (-2.0 / vectors.shape[-1]))
    angles = positions[..., None] * frequency
    cosine = jnp.cos(angles)
    sine_part = jnp.sin(angles)
    lower_half = vectors[..., :half_dim]
    upper_half = vectors[..., half_dim:]
    return jnp.concatenate(
        [
            lower_half * cosine - upper_half * sine_part,
            upper_half * cosine + lower_half * sine_part,
        ],
        axis=-1,
    )


def project_rows(normed, weight_rows):
    return jnp.dot(normed, weight_rows, preferred_element_type=jnp.float32)


def attend_all(rotated, new_keys, new_values, old_keys, old_values, turn_len, cache_len):
    session_count, turn_size, kv_local, head_dim = new_keys.shape
    head_local = rotated.shape[2]
    group_size = head_local // kv_local
    cache_size = old_keys.shape[1]
    factor = head_dim ** (-0.5)
    grouped = rotated.reshape(session_count, turn_size, kv_local, group_size, head_dim)
    far_scores = (
        jnp.einsum("stkgd,slkd->skgtl", grouped, old_keys, preferred_element_type=jnp.float32)
        * factor
    )
    near_scores = (
        jnp.einsum("stkgd,sukd->skgtu", grouped, new_keys, preferred_element_type=jnp.float32)
        * factor
    )
    slot_index = jnp.arange(cache_size, dtype=jnp.int32)
    turn_index = jnp.arange(turn_size, dtype=jnp.int32)
    slot_live = slot_index[None, :] < cache_len[:, None]
    far_scores = jnp.where(slot_live[:, None, None, None, :], far_scores, -jnp.inf)
    near_scores = jnp.where(turn_index[None, :] <= turn_index[:, None], near_scores, -jnp.inf)
    row_max = jnp.maximum(jnp.max(far_scores, axis=-1), jnp.max(near_scores, axis=-1))[..., None]
    far_exp = jnp.exp(far_scores - row_max)
    near_exp = jnp.exp(near_scores - row_max)
    totals = jnp.sum(far_exp, axis=-1, keepdims=True) + jnp.sum(near_exp, axis=-1, keepdims=True)
    far_weights = (far_exp / totals).astype(jnp.bfloat16)
    near_weights = (near_exp / totals).astype(jnp.bfloat16)
    mixed = jnp.einsum(
        "skgtl,slkd->stkgd", far_weights, old_values, preferred_element_type=jnp.float32
    )
    mixed = mixed + jnp.einsum(
        "skgtu,sukd->stkgd", near_weights, new_values, preferred_element_type=jnp.float32
    )
    live_rows = turn_index[None, :] < turn_len[:, None]
    mixed = jnp.where(live_rows[:, :, None, None, None], mixed, 0.0)
    return mixed.reshape(session_count * turn_size, head_local * head_dim).astype(jnp.bfloat16)


def local_gather(tokens, norm_gain, w_query, w_key, w_value, cache_key, cache_value, turn_len, cache_len):
    gathered = lax.all_gather(tokens, "head", axis=1, tiled=True)
    widened = gathered.astype(jnp.float32)
    inverse_rms = lax.rsqrt(jnp.mean(widened * widened, axis=1, keepdims=True) + EPSILON)
    normed = (widened * inverse_rms * norm_gain).astype(jnp.bfloat16)
    row_count = normed.shape[0]
    query_width = w_query.shape[1]
    pair_width = w_key.shape[1]
    queries = project_rows(normed, lax.all_gather(w_query, "wloop", axis=0, tiled=True))
    keys_raw = project_rows(normed, lax.all_gather(w_key, "wloop", axis=0, tiled=True))
    values_raw = project_rows(normed, lax.all_gather(w_value, "wloop", axis=0, tiled=True))
    session_count = turn_len.shape[0]
    turn_size = row_count // session_count
    head_local = query_width // HEAD_DIM
    kv_local = pair_width // HEAD_DIM
    turn_index = jnp.arange(turn_size, dtype=jnp.int32)
    positions = (cache_len[:, None] + turn_index[None, :]).astype(jnp.float32)[:, :, None]
    live_rows = turn_index[None, :] < turn_len[:, None]
    rotated = rotate(
        queries.reshape(session_count, turn_size, head_local, HEAD_DIM), positions
    ).astype(jnp.bfloat16)
    new_keys = jnp.where(
        live_rows[:, :, None, None],
        rotate(keys_raw.reshape(session_count, turn_size, kv_local, HEAD_DIM), positions),
        0.0,
    ).astype(jnp.bfloat16)
    new_values = jnp.where(
        live_rows[:, :, None, None],
        values_raw.reshape(session_count, turn_size, kv_local, HEAD_DIM),
        0.0,
    ).astype(jnp.bfloat16)
    old_keys = cache_key.reshape(session_count, cache_key.shape[1], kv_local, HEAD_DIM)
    old_values = cache_value.reshape(session_count, cache_value.shape[1], kv_local, HEAD_DIM)
    attended = attend_all(rotated, new_keys, new_values, old_keys, old_values, turn_len, cache_len)
    return (
        attended,
        new_keys.reshape(row_count, pair_width),
        new_values.reshape(row_count, pair_width),
    )


def column_of(row):
    lanes = row.shape[1]
    return jnp.transpose(jnp.broadcast_to(row, (lanes, lanes)))[:, :1]


def row_of(column):
    lanes = column.shape[0]
    return jnp.transpose(jnp.broadcast_to(column, (lanes, lanes)))[:8, :]


def move_kernel(
    width,
    tokens_ref,
    gain_ref,
    out_ref,
    stage,
    relay,
    mine,
    sums,
    piece_send,
    piece_recv,
    relay_send,
    relay_recv,
    self_sem,
    sums_send,
    sums_recv,
    pair_send,
    pair_recv,
    cross_send,
    cross_recv,
    pass_send,
    pass_recv,
    own_sem,
):
    ways, rows = stage.shape[0], stage.shape[1]
    w_at, h_at = lax.axis_index("wloop"), lax.axis_index("head")

    def device(w, h):
        return {"wloop": w, "head": h}

    barrier = pltpu.get_barrier_semaphore()
    for dw in range(ways):
        for dh in range(ways):
            if dw or dh:
                pl.semaphore_signal(
                    barrier,
                    inc=1,
                    device_id=device(lax.rem(w_at + dw, ways), lax.rem(h_at + dh, ways)),
                    device_id_type=pl.DeviceIdType.MESH,
                )
    pl.semaphore_wait(barrier, ways * ways - 1)

    def remote(source, target, send, recv, w, h):
        return pltpu.make_async_remote_copy(
            src_ref=source,
            dst_ref=target,
            send_sem=send,
            recv_sem=recv,
            device_id=device(w, h),
            device_id_type=pl.DeviceIdType.MESH,
        )

    sibling = h_at + 1 - 2 * lax.rem(h_at, 2)
    partner = lax.rem(h_at + ways // 2, ways)
    across = lax.rem(sibling + ways // 2, ways)

    def rows_for(h):
        return tokens_ref.at[pl.ds(pl.multiple_of(h * rows, rows), rows), :]

    def to_stage(source, at, w, h):
        return remote(source, stage.at[w_at], piece_send.at[at], piece_recv.at[w_at], w, h)

    crossing = [
        remote(rows_for(h), relay.at[at], relay_send.at[at], relay_recv.at[at], w_at, partner)
        for at, h in enumerate((across, partner))
    ]
    for copy in crossing:
        copy.start()
    beside = to_stage(rows_for(sibling), 0, h_at, sibling)
    beside.start()
    straight = to_stage(rows_for(h_at), 1, h_at, h_at)
    kept = pltpu.make_async_copy(rows_for(h_at), stage.at[w_at], self_sem.at[0])
    relayed_beside = to_stage(relay.at[0], 2, partner, sibling)
    relayed = to_stage(relay.at[1], 3, partner, h_at)
    relay_kept = pltpu.make_async_copy(relay.at[1], stage.at[w_at], self_sem.at[1])

    @pl.when(w_at != h_at)
    def _():
        straight.start()

    @pl.when(w_at == h_at)
    def _():
        kept.start()

    crossing[0].wait_recv()
    relayed_beside.start()
    crossing[1].wait_recv()

    @pl.when(w_at != partner)
    def _():
        relayed.start()

    @pl.when(w_at == partner)
    def _():
        relay_kept.start()

    def arrival(block):
        return pltpu.make_async_remote_copy(
            src_ref=stage.at[block],
            dst_ref=stage.at[block],
            send_sem=piece_send.at[0],
            recv_sem=piece_recv.at[block],
            device_id=device(w_at, sibling),
            device_id_type=pl.DeviceIdType.MESH,
        )

    def block_of(j):
        return lax.rem(h_at + ways - j, ways)

    exchanges = [
        [
            remote(
                sums.at[j, w_at],
                sums.at[j, w_at],
                sums_send.at[j, k - 1],
                sums_recv.at[j, k - 1],
                lax.rem(w_at + k, ways),
                h_at,
            )
            for k in range(1, ways)
        ]
        for j in range(ways)
    ]
    sends = []
    for j in range(ways):
        block = block_of(j)
        sends.append(
            (
                pltpu.make_async_copy(mine.at[block], out_ref.at[block, h_at], own_sem.at[j]),
                remote(
                    mine.at[block],
                    out_ref.at[block, h_at],
                    cross_send.at[j],
                    cross_recv.at[j],
                    w_at,
                    partner,
                ),
                remote(
                    mine.at[block],
                    out_ref.at[block, h_at],
                    pair_send.at[j],
                    pair_recv.at[j],
                    w_at,
                    sibling,
                ),
            )
        )

    def take_in(j):
        block = block_of(j)
        own = jnp.logical_and(block == w_at, lax.rem(h_at, ways // 2) == lax.rem(w_at, ways // 2))

        @pl.when(jnp.logical_not(own))
        def _():
            arrival(block).wait_recv()

        @pl.when(jnp.logical_and(own, w_at == h_at))
        def _():
            kept.wait()

        @pl.when(jnp.logical_and(own, w_at != h_at))
        def _():
            relay_kept.wait()

        held = stage[block].astype(jnp.float32)
        total = jnp.sum(held * held, axis=1, keepdims=True)
        sums[j, w_at] = row_of(total)
        for exchange in exchanges[j]:
            exchange.start()

    def give_out(j):
        for exchange in exchanges[j]:
            exchange.wait_recv()
        total = sums[j, 0]
        for w in range(1, ways):
            total = total + sums[j, w]
        inverse = column_of(lax.rsqrt(total[:1] / width + EPSILON))
        block = block_of(j)
        held = stage[block].astype(jnp.float32)
        mine[block] = (held * inverse * gain_ref[...]).astype(jnp.bfloat16)
        for copy in reversed(sends[j]):
            copy.start()

    take_in(0)
    for j in range(1, ways):
        take_in(j)
        give_out(j - 1)
    give_out(ways - 1)

    passes = []
    for j in range(ways):
        block = lax.rem(partner + ways - j, ways)
        sends[j][1].wait_recv()
        passed = remote(
            out_ref.at[block, partner],
            out_ref.at[block, partner],
            pass_send.at[j],
            pass_recv.at[j],
            w_at,
            sibling,
        )
        passed.start()
        passes.append(passed)
    for j in range(ways):
        sends[j][0].wait()
        sends[j][1].wait_send()
        sends[j][2].wait()
        passes[j].wait()
        for exchange in exchanges[j]:
            exchange.wait_send()
    beside.wait_send()
    relayed_beside.wait_send()
    for copy in crossing:
        copy.wait_send()

    @pl.when(w_at != h_at)
    def _():
        straight.wait_send()

    @pl.when(w_at != partner)
    def _():
        relayed.wait_send()


def moved_normed(tokens, gain, width, ways):
    row_count, depth = tokens.shape
    rows = row_count // ways
    pair = pltpu.SemaphoreType.DMA((ways,))
    grid = pltpu.SemaphoreType.DMA((ways, ways - 1))
    moved = pl.pallas_call(
        functools.partial(move_kernel, width),
        out_shape=jax.ShapeDtypeStruct((ways, ways, rows, depth), jnp.bfloat16),
        in_specs=[
            pl.BlockSpec(memory_space=pl.ANY),
            pl.BlockSpec(memory_space=pltpu.VMEM),
        ],
        out_specs=pl.BlockSpec(memory_space=pl.ANY),
        scratch_shapes=[
            pltpu.VMEM((ways, rows, depth), jnp.bfloat16),
            pltpu.VMEM((2, rows, depth), jnp.bfloat16),
            pltpu.VMEM((ways, rows, depth), jnp.bfloat16),
            pltpu.VMEM((ways, ways, 8, rows), jnp.float32),
            pair,
            pair,
            pltpu.SemaphoreType.DMA((2,)),
            pltpu.SemaphoreType.DMA((2,)),
            pltpu.SemaphoreType.DMA((2,)),
            grid,
            grid,
            pair,
            pair,
            pair,
            pair,
            pair,
            pair,
            pair,
        ],
        compiler_params=pltpu.CompilerParams(
            collective_id=0, has_side_effects=True, vmem_limit_bytes=24 * 1024 * 1024
        ),
    )(tokens, gain.reshape(1, depth))
    return moved.reshape(ways, row_count, depth)


def attend_kernel(
    group_size, turn_len_ref, cache_len_ref, q_ref, kv_ref, cos_ref, sin_ref, old_k_ref, old_v_ref,
    *rest,
):
    out_ref, new_k_ref, new_v_ref = rest[-3:]
    at = pl.program_id(0)
    turn_size, head_dim = cos_ref.shape
    cache_size = old_k_ref.shape[1]
    cosine, sine = cos_ref[...], sin_ref[...]

    def turned(v):
        return v * cosine + pltpu.roll(v, head_dim // 2, 1) * sine

    live = lax.broadcasted_iota(jnp.int32, (turn_size, head_dim), 0) < turn_len_ref[at]
    new_k = jnp.where(live, turned(kv_ref[:, :head_dim]), 0.0).astype(jnp.bfloat16)
    new_v = jnp.where(live, kv_ref[:, head_dim:], 0.0).astype(jnp.bfloat16)
    new_k_ref[...] = new_k
    new_v_ref[...] = new_v
    old_k, old_v = old_k_ref[0], old_v_ref[0]
    slot_live = lax.broadcasted_iota(jnp.int32, (1, cache_size), 1) < cache_len_ref[at]
    bias = jnp.where(slot_live, 0.0, -jnp.inf)
    stack = 2 if group_size % 2 == 0 else 1
    causal = lax.broadcasted_iota(jnp.int32, (turn_size, turn_size), 1) <= (
        lax.broadcasted_iota(jnp.int32, (turn_size, turn_size), 0)
    )
    near_bias = jnp.concatenate([jnp.where(causal, 0.0, -jnp.inf)] * stack, axis=0)
    factor = head_dim ** (-0.5)
    contract = (((1,), (1,)), ((), ()))
    for first in range(0, group_size, stack):
        cols = [slice(h * head_dim, (h + 1) * head_dim) for h in range(first, first + stack)]
        query = jnp.concatenate([turned(q_ref[:, c]) for c in cols], axis=0).astype(jnp.bfloat16)
        far = lax.dot_general(query, old_k, contract, preferred_element_type=jnp.float32)
        near = lax.dot_general(query, new_k, contract, preferred_element_type=jnp.float32)
        far = far * factor + bias
        near = near * factor + near_bias
        top = jnp.maximum(
            jnp.max(far, axis=1, keepdims=True), jnp.max(near, axis=1, keepdims=True)
        )
        far = jnp.exp(far - top)
        near = jnp.exp(near - top)
        total = jnp.sum(far, axis=1, keepdims=True) + jnp.sum(near, axis=1, keepdims=True)
        mixed = jnp.dot(
            far.astype(jnp.bfloat16), old_v, preferred_element_type=jnp.float32
        ) + jnp.dot(near.astype(jnp.bfloat16), new_v, preferred_element_type=jnp.float32)
        mixed = mixed * (1.0 / total)
        for at, c in enumerate(cols):
            block = mixed[at * turn_size : (at + 1) * turn_size]
            out_ref[:, c] = jnp.where(live, block, 0.0).astype(jnp.bfloat16)


def attend_part(
    summed, cosine, sine, cache_key, cache_value, turn_len, cache_len, kv, kv_local, filled
):
    row_count, width = summed.shape
    sessions, cache_size, _ = cache_key.shape
    turn_size = row_count // sessions
    q_cols = width - 2 * HEAD_DIM
    smem = pl.BlockSpec(memory_space=pltpu.SMEM)
    rows = lambda cols, at=0: pl.BlockSpec((turn_size, cols), lambda s: (s, at))
    cached = pl.BlockSpec((1, cache_size, HEAD_DIM), lambda s: (s, 0, kv))
    bf16 = lambda cols: jax.ShapeDtypeStruct((row_count, kv_local * cols), jnp.bfloat16)
    filled = filled or ()
    anywhere = pl.BlockSpec(memory_space=pl.ANY)
    work = row_count * q_cols * (cache_size + turn_size)
    return pl.pallas_call(
        functools.partial(attend_kernel, q_cols // HEAD_DIM),
        grid=(sessions,),
        out_shape=(bf16(q_cols), bf16(HEAD_DIM), bf16(HEAD_DIM)),
        in_specs=[
            smem,
            smem,
            rows(q_cols),
            rows(2 * HEAD_DIM, q_cols // (2 * HEAD_DIM)),
            rows(HEAD_DIM),
            rows(HEAD_DIM),
            cached,
            cached,
            *([anywhere] * len(filled)),
        ],
        out_specs=(rows(q_cols, kv), rows(HEAD_DIM, kv), rows(HEAD_DIM, kv)),
        input_output_aliases={8 + at: at for at in range(len(filled))},
        compiler_params=pltpu.CompilerParams(vmem_limit_bytes=32 * 1024 * 1024),
        cost_estimate=pl.CostEstimate(
            flops=16 * work, bytes_accessed=10**7, transcendentals=work // HEAD_DIM
        ),
    )(turn_len, cache_len, summed, summed, cosine, sine, cache_key, cache_value, *filled)


def reduce_over_line(normed, weights, ways):
    w_at = lax.axis_index("wloop")

    def times(rows, spec):
        return [
            jnp.einsum(spec, rows, w, preferred_element_type=jnp.float32)[..., kept]
            for w, kept in weights
        ]

    first_at = jnp.where(w_at == 0, ways - 1, 0)
    first_rows = lax.dynamic_index_in_dim(normed, first_at, 0, keepdims=False)
    first = jnp.concatenate(
        [part.astype(jnp.bfloat16) for part in times(first_rows, "rd,dn->rn")], axis=1
    )
    rising = lax.ppermute(first, "wloop", [(0, 1)])
    falling = lax.ppermute(first, "wloop", [(ways - 1, ways - 2)])
    partials = times(normed, "brd,dn->brn")

    def pick(index):
        index = jnp.clip(index, 0, ways - 1)
        return jnp.concatenate(
            [lax.dynamic_index_in_dim(part, index, 0, keepdims=False) for part in partials], axis=1
        )

    for step in range(2, ways):
        up = pick(w_at + ways - step) + rising.astype(jnp.float32)
        down = pick(w_at - ways + step) + falling.astype(jnp.float32)
        rising = lax.ppermute(
            up.astype(jnp.bfloat16), "wloop", [(w, w + 1) for w in range(step)]
        )
        falling = lax.ppermute(
            down.astype(jnp.bfloat16), "wloop", [(ways - 1 - w, ways - 2 - w) for w in range(step)]
        )
    return pick(w_at) + rising.astype(jnp.float32) + falling.astype(jnp.float32)


def local_reduce(
    tokens, norm_gain, w_query, w_key, w_value, cache_key, cache_value, turn_len, cache_len
):
    ways = lax.axis_size("wloop")
    row_count = tokens.shape[0]
    depth = w_query.shape[0]
    width = norm_gain.shape[0]
    kv_local = w_key.shape[1] // HEAD_DIM
    q_cols = w_query.shape[1] // kv_local
    turn_size = row_count // turn_len.shape[0]
    w_at = lax.axis_index("wloop")

    gain = lax.dynamic_slice_in_dim(norm_gain, w_at * depth, depth, 0)
    normed = moved_normed(tokens, gain, width, ways)

    half_dim = HEAD_DIM // 2
    freq_index = jnp.arange(half_dim, dtype=jnp.float32)
    frequency = jnp.power(jnp.float32(THETA), freq_index * (-2.0 / HEAD_DIM))
    turn_index = jnp.arange(turn_size, dtype=jnp.int32)
    positions = (cache_len[:, None] + turn_index[None, :]).astype(jnp.float32)
    angles = positions.reshape(row_count, 1) * frequency
    cosine, sine = jnp.cos(angles), jnp.sin(angles)
    cosine = jnp.concatenate([cosine, cosine], axis=1)
    sine = jnp.concatenate([-sine, sine], axis=1)

    outs = None
    for kv in range(kv_local):
        heads = slice(kv * HEAD_DIM, (kv + 1) * HEAD_DIM)
        weights = (
            (w_query[:, kv * q_cols : (kv + 1) * q_cols], slice(None)),
            (w_key, heads),
            (w_value, heads),
        )
        summed = reduce_over_line(normed, weights, ways)
        outs = attend_part(
            summed, cosine, sine, cache_key, cache_value, turn_len, cache_len, kv, kv_local, outs
        )
    return outs


def local(*args):
    tokens, norm_gain = args[0], args[1]
    w_ways, h_ways = lax.axis_size("wloop"), lax.axis_size("head")
    if w_ways == h_ways == 4 and tokens.shape[0] == w_ways * HEAD_DIM:
        if w_ways * tokens.shape[0] < norm_gain.shape[0]:
            return local_reduce(*args)
    return local_gather(*args)


def solution(mesh):
    placed = (
        P(("grp", "wloop"), "head"),
        P(),
        P("wloop", "head"),
        P("wloop", "head"),
        P("wloop", "head"),
        P(("grp", "wloop"), None, "head"),
        P(("grp", "wloop"), None, "head"),
        P(("grp", "wloop")),
        P(("grp", "wloop")),
    )
    return jax.shard_map(
        local,
        mesh=mesh,
        in_specs=placed,
        out_specs=(
            P(("grp", "wloop"), "head"),
            P(("grp", "wloop"), "head"),
            P(("grp", "wloop"), "head"),
        ),
        check_vma=False,
    )
```
